32 devices in a mesh: groups: 2 (over y), dp: 4 (over z), tensor: 4 (over x, core).
Axes of the slice: x: 2, y: 2, z: 4, core: 2. Of those that a mesh axis runs over, the one named last changes fastest.
Arguments:
- hidden_rows: bfloat16 [4096, 3, 8192], P(('groups', 'dp'), None, 'tensor'), parts along dimension 0, may hold values from -120 to 120
- layer_gain: float32 [3, 8192], P(None, 'tensor'), may hold values from 0.1 to 1.9
- key_weight: bfloat16 [8192, 1024], P(('tensor', 'dp')), may hold values from -0.0625 to 0.0625
- step_decay: float32 [1024], P('tensor'), may hold values from 0.3 to 1
- owner_list: int32 [256], P('groups'), parts along dimension 0, may hold values from 0 to 3, as said below
- segment_len: int32 [256], P('groups'), parts along dimension 0, may hold values from 1 to 16
- reweight_count: int32 [256], P('groups'), parts along dimension 0, may hold values from 1 to 4
- loss_mask: int32 [4096], P('groups'), parts along dimension 0, may hold values 0 or 1
- state_cotangent: bfloat16 [3, 256, 16, 1024], P(None, ('groups', 'dp'), None, 'tensor'), parts along dimension 1, may hold values from -0.125 to 0.125
Outputs:
- states: bfloat16 [3, 256, 16, 1024], P(None, ('groups', 'dp'), None, 'tensor'), parts along dimension 1
- weight_grad: float32 [16384, 1024], P(('groups', 'tensor', 'dp')), parts along dimension 0
The draws below stay inside these ranges and needn't reach their ends.
There are 2 independent parts, one for each index of `groups`. The reference program is written for one: setup_inputs(seed, part) draws one part's arguments, and reference() takes and returns one part's arrays. A program takes and returns all parts, laid end to end along the dimension named above; an argument that names none is the same for every part. Nothing has to cross between parts.
Inputs may be any that keep to these rules, and one draw needn't show every extreme that they name: `owner_list`: every owner receives exactly 32 segments in all; at most 16 segments of one index of dp share an owner, and exactly 16 for some pair in every draw.
All inputs are finite; a program needn't handle non-finite values.
Results may differ from the reference program's by a relative error of at most 0.0049.
Values may be sent and summed in bfloat16 or wider, within the bound.
A program may use at most 128 MiB of HBM per device.

```python
import math
import jax
import jax.numpy as jnp
from jax import lax

D = 8192
KW = 1024
SEG = 16
SEG_DEV = 32
SEG_CAP = 16
TOK_DEV = 512
TOKENS = 2048
SEGS = 128
N_DP = 4


def draw_hidden_rows(key, part):
    key = jax.random.fold_in(key, 5)
    subkeys = jax.random.split(key, 3)
    normal_part = jnp.clip(jax.random.normal(subkeys[0], (TOKENS, 3, D), jnp.float32), -4.0, 4.0)
    column = jnp.exp(jnp.log(3.0) * jnp.arange(D, dtype=jnp.float32) / D + jnp.log(10.0) * jax.random.uniform(subkeys[1], (3, D), jnp.float32))
    rowscale = jnp.exp(jnp.log(10.0) * jax.random.uniform(subkeys[2], (TOKENS, 3, 1), jnp.float32))
    return (0.1 * normal_part * column * rowscale).astype(jnp.bfloat16)


def draw_owner_list(key, part):
    key = jax.random.fold_in(key, 11)
    subkeys = jax.random.split(key, 5)
    offset_order = jax.random.permutation(subkeys[0], N_DP)
    remaining = jax.random.permutation(subkeys[1], N_DP * SEG_CAP - SEG_CAP) + SEG_CAP
    chosen = jnp.concatenate([jnp.arange(SEG_CAP), remaining[:SEG_DEV - SEG_CAP]])
    offsets = offset_order[chosen // SEG_CAP]
    offsets = offsets[jax.random.permutation(subkeys[2], SEG_DEV)]
    source_order = jax.random.permutation(subkeys[3], N_DP)
    owner_order = jax.random.permutation(subkeys[4], N_DP)
    owners = owner_order[(source_order[:, None] + offsets[None, :]) % N_DP]
    return owners.reshape(-1).astype(jnp.int32)


def plant(entries, rng, smallest, largest):
    spot = [jax.random.randint(jax.random.fold_in(rng, axis), (), 0, length) for axis, length in enumerate(entries.shape)]
    longest = entries.shape.index(max(entries.shape))
    next_to = spot[:longest] + [(spot[longest] + 1) % entries.shape[longest]] + spot[longest + 1:]
    return entries.at[tuple(spot)].set(smallest).at[tuple(next_to)].set(largest)


def block_scale(own_key, dims, cuts, least, largest):
    gain, own = 1.0, jax.random.fold_in(own_key, 6)
    for position, shards_of in cuts:
        draws = jnp.exp(jax.random.uniform(jax.random.fold_in(own, position), (shards_of,), jnp.float32, least / len(cuts), largest / len(cuts)))
        gain = gain * jnp.repeat(draws, dims[position] // shards_of).reshape([-1 if axis == position else 1 for axis in range(len(dims))])
    return gain


def bell_draw(rng, shape, spread, reach, shards=(), kind=jnp.bfloat16):
    loudness = block_scale(rng, shape, shards, -0.22, 0.18) if shards else 1.0
    result = jax.random.normal(rng, shape, jnp.float32) * spread * loudness
    return jnp.minimum(jnp.maximum(result, -reach), reach).astype(kind)


def setup_inputs(seed: int = 0, part: int = 0) -> dict:
    key_of = jax.random.split(jax.random.key(seed), 10)
    own_keys = jax.random.split(jax.random.fold_in(key_of[9], part), 10)
    return {
        "hidden_rows": draw_hidden_rows(jax.random.fold_in(jax.random.fold_in(key_of[9], part), 71), part),
        "layer_gain": jnp.clip(1.0 + 0.18 * jax.random.normal(key_of[1], (3, D), jnp.float32), 0.1, 1.9),
        "key_weight": bell_draw(key_of[2], (D, KW), D ** -0.5, 0.0625, ((0, 16),)),
        "step_decay": jnp.clip(jnp.exp(math.log(1.0) - 1.2039728 * jax.random.uniform(key_of[3], (KW,), jnp.float32) ** block_scale(key_of[3], (KW,), ((0, 4),), -0.2, 0.2)), 0.3, 1.0),
        "owner_list": draw_owner_list(jax.random.fold_in(jax.random.fold_in(key_of[9], part), 71), part),
        "segment_len": plant(jax.random.randint(own_keys[5], (SEGS,), 1, SEG + 1), jax.random.fold_in(own_keys[5], 1), 1, SEG).astype(jnp.int32),
        "reweight_count": plant(jax.random.randint(own_keys[6], (SEGS,), 1, 5), jax.random.fold_in(own_keys[6], 1), 1, 4).astype(jnp.int32),
        "loss_mask": plant((jax.random.randint(own_keys[7], (TOKENS,), 0, 4) < 3).astype(jnp.int32), jax.random.fold_in(own_keys[7], 1), 0, 1),
        "state_cotangent": bell_draw(own_keys[8], (3, SEGS, SEG, KW), TOKENS ** -0.5, 0.125, ((1, 4), (3, 4))),
    }


epsilon = 1e-05

def join_block(row_block, live_block, layer_gain):
    values = row_block.astype(jnp.float32)
    squares = lax.optimization_barrier(jnp.sum(values * values, axis=-1))
    inverse = lax.rsqrt(squares / D + epsilon)
    mixture = lax.optimization_barrier(jnp.sum(values * layer_gain[None] * inverse[..., None], axis=1))
    return (mixture * live_block[:, None]).astype(jnp.bfloat16)

def shift_down(values):
    zeros = jnp.zeros_like(values[:, :1])
    return jnp.concatenate([zeros, values[:, :-1]], axis=1)

def shift_up(values):
    zeros = jnp.zeros_like(values[:, :1])
    return jnp.concatenate([values[:, 1:], zeros], axis=1)

def reference(hidden_rows, layer_gain, key_weight, step_decay, owner_list, segment_len, reweight_count, loss_mask, state_cotangent):
    segment_count = N_DP * SEG_DEV
    positions = (jnp.arange(TOKENS) % SEG).astype(jnp.int32)
    token_len = jnp.repeat(segment_len, SEG)
    live_mask = (positions < token_len).astype(jnp.float32)

    def join_pair(block_pair):
        return join_block(block_pair[0], block_pair[1], layer_gain)
    joined_rows = lax.map(join_pair, (hidden_rows.reshape(N_DP, TOK_DEV, 3, D), live_mask.reshape(N_DP, TOK_DEV)))
    joined_rows = joined_rows.reshape(TOKENS, D)
    key_rows = jnp.dot(joined_rows, key_weight, preferred_element_type=jnp.float32).reshape(segment_count, SEG, KW)
    first = key_rows
    second = key_rows + step_decay * shift_down(first)
    third = key_rows + step_decay * shift_down(second)
    source_states = jnp.stack([first, second, third])
    segment_ids = jnp.arange(segment_count).astype(jnp.int32)
    same_owner = owner_list[None, :] == owner_list[:, None]
    earlier = segment_ids[None, :] < segment_ids[:, None]
    rank_ids = lax.optimization_barrier(jnp.sum(same_owner & earlier, axis=1)).astype(jnp.int32)
    destination = (owner_list * SEG_DEV + rank_ids).astype(jnp.int32)
    source_of = jnp.zeros((segment_count,), jnp.int32).at[destination].set(segment_ids)
    states = source_states[:, source_of].astype(jnp.bfloat16)
    scale_rows = loss_mask.reshape(segment_count, SEG).astype(jnp.float32) * reweight_count.astype(jnp.float32)[:, None]
    state_grads = state_cotangent[:, destination].astype(jnp.float32) * scale_rows[None, :, :, None]
    grad_third = state_grads[2]
    grad_second = state_grads[1] + step_decay * shift_up(grad_third)
    grad_first = state_grads[0] + step_decay * shift_up(grad_second)
    key_grads = (grad_first + grad_second + grad_third).astype(jnp.bfloat16).reshape(TOKENS, KW)
    weight_grad = lax.dot_general(joined_rows, key_grads, (((0,), (0,)), ((), ())), preferred_element_type=jnp.float32)
    return (states, weight_grad)
```

```python
import jax
import jax.numpy as jnp
from jax import lax
from jax.experimental import pallas as pl
from jax.experimental.pallas import tpu as pltpu
from jax.sharding import PartitionSpec as P

D = 8192
SEG = 16
SEG_DEV = 32


epsilon = 1e-05


def shift_down(values):
    zeros = jnp.zeros_like(values[:, :1])
    return jnp.concatenate([zeros, values[:, :-1]], axis=1)


def shift_up(values):
    zeros = jnp.zeros_like(values[:, :1])
    return jnp.concatenate([values[:, 1:], zeros], axis=1)


def unrolled_steps(key_rows, decay_part):
    second = key_rows + decay_part * shift_down(key_rows)
    third = key_rows + decay_part * shift_down(second)
    return jnp.stack([key_rows, second, third])


def unrolled_grads(state_grads, decay_part):
    grad_third = state_grads[2]
    grad_second = state_grads[1] + decay_part * shift_up(grad_third)
    grad_first = state_grads[0] + decay_part * shift_up(grad_second)
    return grad_first + grad_second + grad_third


def layer_squares(row_block):
    values = row_block.astype(jnp.float32)
    return jnp.sum(values * values, axis=-1)


def normalize(row_block, squares, live_mask, layer_gain):
    inverse = lax.rsqrt(squares / D + epsilon)
    mixture = jnp.sum(row_block.astype(jnp.float32) * layer_gain * inverse[..., None], axis=2)
    return (mixture * live_mask[..., None]).astype(jnp.bfloat16)


def per_device(
    hidden_rows,
    layer_gain,
    key_weight,
    step_decay,
    owner_list,
    segment_len,
    reweight_count,
    loss_mask,
    state_cotangent,
):
    dp_count = lax.axis_size("dp")
    dp_index = lax.axis_index("dp")
    tp_index = lax.axis_index("tensor")
    part_width = hidden_rows.shape[2]
    key_width = key_weight.shape[1]
    share_width = state_cotangent.shape[3]
    capacity = max(2, (2 * SEG_DEV + dp_count - 1) // dp_count)
    slot_total = dp_count * capacity
    owner_table = owner_list.reshape(dp_count, SEG_DEV)
    positions = jnp.arange(SEG)
    segment_ids = jnp.arange(dp_count * SEG_DEV)
    local_ids = jnp.arange(SEG_DEV)
    slot_ids = jnp.arange(slot_total)
    zero_value = jnp.zeros((), jnp.bfloat16)
    my_owners = lax.dynamic_index_in_dim(owner_table, dp_index, 0, keepdims=False)
    earlier = (my_owners[None, :] == my_owners[:, None]) & (local_ids[None, :] < local_ids[:, None])
    slot_out = my_owners * capacity + jnp.sum(earlier, axis=1)
    out_match = slot_ids[:, None] == slot_out[None, :]
    send_pick = jnp.sum(jnp.where(out_match, local_ids[None, :], 0), axis=1)
    send_used = jnp.any(out_match, axis=1)
    incoming = owner_table == dp_index
    flat_in = incoming.reshape(-1)
    rank_flat = jnp.cumsum(flat_in.astype(jnp.int32)) - 1
    within_src = (jnp.cumsum(incoming.astype(jnp.int32), axis=1) - 1).reshape(-1)
    chosen = (rank_flat[None, :] == local_ids[:, None]) & flat_in[None, :]
    global_seg = jnp.sum(jnp.where(chosen, segment_ids[None, :], 0), axis=1)
    slot_in = jnp.sum(
        jnp.where(chosen, (segment_ids // SEG_DEV * capacity + within_src)[None, :], 0), axis=1
    )
    live_owner = (positions[None, :] < segment_len[global_seg][:, None]).astype(jnp.float32)
    mask_table = loss_mask.reshape(dp_count * SEG_DEV, SEG).astype(jnp.float32)
    weight_table = reweight_count.astype(jnp.float32)
    scale_owner = mask_table[global_seg] * weight_table[global_seg][:, None]
    row_block = hidden_rows.reshape(SEG_DEV, SEG, hidden_rows.shape[1], part_width)
    outgoing = jnp.where(send_used[:, None, None, None], row_block[send_pick], zero_value)
    arrived = lax.all_to_all(outgoing, "dp", split_axis=0, concat_axis=0, tiled=True)
    owner_rows = arrived[slot_in]
    squares = lax.psum(layer_squares(owner_rows), "tensor")
    joined_rows = normalize(owner_rows, squares, live_owner, layer_gain)
    flat_rows = joined_rows.reshape(-1, part_width)
    columns = flat_rows
    partial_keys = jnp.dot(
        columns,
        lax.all_gather(key_weight, "dp", axis=0, tiled=True),
        preferred_element_type=jnp.float32,
    )
    summed_keys = lax.psum(partial_keys, "tensor")
    key_share = lax.dynamic_slice_in_dim(summed_keys, tp_index * share_width, share_width, 1)
    states = unrolled_steps(key_share.reshape(SEG_DEV, SEG, share_width), step_decay).astype(
        jnp.bfloat16
    )
    state_grads = state_cotangent.astype(jnp.float32) * scale_owner[None, :, :, None]
    key_grads = unrolled_grads(state_grads, step_decay).astype(jnp.bfloat16)
    all_grads = lax.all_gather(key_grads, "tensor", axis=2, tiled=True)
    flat_grads = all_grads.reshape(-1, key_width)
    weight_flat_rows = joined_rows.reshape(-1, part_width)
    columns = weight_flat_rows
    weight_grad = lax.psum_scatter(
        lax.dot_general(
            columns, flat_grads, (((0,), (0,)), ((), ())), preferred_element_type=jnp.float32
        ),
        "dp",
        scatter_dimension=0,
        tiled=True,
    )
    return (states, weight_grad)


N_DP = 4
N_TP = 4
CHUNK = 128
BF16 = jnp.bfloat16
F32 = jnp.float32


def fused_kernel(
    dest_ref,
    hidden_ref,
    gain_ref,
    live_ref,
    weight_ref,
    decay_ref,
    grads_ref,
    states_ref,
    wgrad_ref,
    hid,
    sqcol,
    sqsend,
    sqrecv,
    invcol,
    jloc,
    jfeat,
    jown,
    jturn,
    order,
    gbuf,
    psend,
    precv,
    pown,
    xsend,
    xrecv,
    keys,
    keysb,
    ksend,
    krecv,
    hid_sem,
    sq_ss,
    sq_rs,
    j_ss,
    j_rs,
    gz_ss,
    gz_rs,
    gx_ss,
    gx_rs,
    gc_ss,
    gc_rs,
    kc_ss,
    kc_rs,
    kx_ss,
    kx_rs,
    kz_ss,
    kz_rs,
):
    z = lax.axis_index("dp")
    t = lax.axis_index("tensor")
    x = t // 2
    c = t % 2
    t_x = (t + 2) % N_TP
    t_c = t + 1 - 2 * c
    t_xc = (t_c + 2) % N_TP
    tokens = hid.shape[1]
    feats = weight_ref.shape[0]
    share = grads_ref.shape[1]
    n_chunk = tokens // CHUNK

    def zto(k):
        return (z + k) % N_DP

    def zfrom(k):
        return (z + N_DP - k) % N_DP

    def lanes(index, width):
        return pl.ds(pl.multiple_of(index * width, width), width)

    def send(src, dst, ss, rs, where):
        return pltpu.make_async_remote_copy(
            src_ref=src,
            dst_ref=dst,
            send_sem=ss,
            recv_sem=rs,
            device_id=where,
            device_id_type=pl.DeviceIdType.MESH,
        )

    def hid_copy(i):
        rows = pl.ds(i * CHUNK, CHUNK)
        return pltpu.make_async_copy(hidden_ref.at[:, rows], hid.at[:, rows], hid_sem.at[i])

    for i in range(n_chunk):
        hid_copy(i).start()

    barrier = pltpu.get_barrier_semaphore()
    for k in range(1, N_DP):
        pl.semaphore_signal(
            barrier, inc=1, device_id={"dp": zto(k)}, device_id_type=pl.DeviceIdType.MESH
        )
    for k in range(1, N_TP):
        pl.semaphore_signal(
            barrier,
            inc=1,
            device_id={"tensor": (t + k) % N_TP},
            device_id_type=pl.DeviceIdType.MESH,
        )
    pl.semaphore_wait(barrier, N_DP + N_TP - 2)

    def g_block(zi, ti):
        return gbuf.at[zi, :, lanes(ti, share)]

    def gz(k):
        return send(
            grads_ref, g_block(z, t), gz_ss.at[k - 1], gz_rs.at[k - 1], {"dp": zto(k)}
        )

    def gx(k):
        block = g_block(zfrom(k), t)
        return send(block, block, gx_ss.at[k], gx_rs.at[k], {"tensor": t_x})

    def gc(k):
        block = g_block(zfrom(k), t)
        return send(block, block, gc_ss.at[k], gc_rs.at[k], {"tensor": t_c})

    def gxc(k):
        block = g_block(zfrom(k), t_x)
        return send(block, block, gc_ss.at[4 + k], gc_rs.at[4 + k], {"tensor": t_c})

    def gz_arrived(k):
        block = g_block(zfrom(k), t)
        return send(block, block, gz_ss.at[k - 1], gz_rs.at[k - 1], {"dp": zto(k)})

    def gx_arrived(k):
        block = g_block(zfrom(k), t_x)
        return send(block, block, gx_ss.at[k], gx_rs.at[k], {"tensor": t_x})

    def gc_arrived(k, ti):
        block = g_block(zfrom(k % 4), ti)
        return send(block, block, gc_ss.at[k], gc_rs.at[k], {"tensor": t_c})

    gbuf[z, :, lanes(t, share)] = grads_ref[...]
    for k in range(1, N_DP):
        gz(k).start()
    gx(0).start()
    gc(0).start()

    lane = lax.broadcasted_iota(jnp.int32, (32, 128), 1)
    for i in range(n_chunk):
        hid_copy(i).wait()

        @pl.loop(0, CHUNK // 32)
        def _(r, i=i):
            rows = pl.ds(pl.multiple_of(i * CHUNK + r * 32, 32), 32)
            sums = []
            for layer in range(3):
                values = hid[layer, rows, :].astype(F32)
                sums.append(jnp.sum(values * values, axis=-1, keepdims=True))
            sqcol[rows, :] = jnp.where(
                lane == 0, sums[0], jnp.where(lane == 1, sums[1], sums[2])
            )

    sqsend[...] = sqcol[...].T[:8]

    def sq(k):
        return send(
            sqsend,
            sqrecv.at[k - 1],
            sq_ss.at[k - 1],
            sq_rs.at[k - 1],
            {"tensor": (t + k) % N_TP},
        )

    for k in range(1, N_TP):
        sq(k).start()
    for k in range(1, N_TP):
        sq(k).wait_recv()
    total = sqsend[...] + sqrecv[0] + sqrecv[1] + sqrecv[2]
    inverse = lax.rsqrt(total / D + epsilon) * live_ref[...]
    invcol[...] = jnp.concatenate([inverse, jnp.zeros((120, tokens), F32)], axis=0).T

    def jsend(k, i):
        rows = pl.ds(i * CHUNK, CHUNK)
        return send(
            jloc.at[k - 1, rows],
            jfeat.at[pl.ds(pl.multiple_of(z * tokens + i * CHUNK, CHUNK), CHUNK)],
            j_ss.at[k - 1, i],
            j_rs.at[k - 1, i],
            {"dp": zto(k)},
        )

    def jarrived(k, i):
        rows = pl.ds(pl.multiple_of(zfrom(k) * tokens + i * CHUNK, CHUNK), CHUNK)
        return send(
            jfeat.at[rows], jfeat.at[rows], j_ss.at[k - 1, i], j_rs.at[k - 1, i], {"dp": zto(k)}
        )

    for i in range(n_chunk):
        for k in (1, 2, 3, 0):
            cols = lanes(zto(k), feats)

            @pl.loop(0, CHUNK // 16)
            def _(r, i=i, k=k, cols=cols):
                rows = pl.ds(pl.multiple_of(i * CHUNK + r * 16, 16), 16)
                factors = invcol[rows, :]
                mixture = jnp.zeros((16, feats), F32)
                for layer in range(3):
                    scaled = hid[layer, rows, cols].astype(F32) * gain_ref[pl.ds(layer, 1), cols]
                    mixture = mixture + scaled * factors[:, layer : layer + 1]
                if k:
                    jloc[k - 1, rows, :] = mixture.astype(BF16)
                else:
                    mine = pl.ds(pl.multiple_of(z * tokens + i * CHUNK + r * 16, 16), 16)
                    jfeat[mine, :] = mixture.astype(BF16)

            if k:
                jsend(k, i).start()

    def kc(k):
        return send(psend.at[k], precv.at[k], kc_ss.at[k], kc_rs.at[k], {"tensor": t_c})

    def kx(k):
        return send(xsend.at[k], xrecv.at[k], kx_ss.at[k], kx_rs.at[k], {"tensor": t_x})

    def project(k):
        if k:
            for i in range(n_chunk):
                jarrived(k, i).wait_recv()

        @pl.loop(0, n_chunk)
        def _(r):
            rows = pl.ds(pl.multiple_of(r * CHUNK, CHUNK), CHUNK)
            source = pl.ds(pl.multiple_of(zfrom(k) * tokens + r * CHUNK, CHUNK), CHUNK)
            block = jfeat[source, :]
            for half in range(2):
                other = weight_ref[:, lanes(2 * half + 1 - c, share)]
                psend[k, half, rows, :] = jnp.dot(
                    block, other, preferred_element_type=F32
                ).astype(BF16)
            for half in range(2):
                own = weight_ref[:, lanes(2 * half + c, share)]
                pown[k, half, rows, :] = jnp.dot(block, own, preferred_element_type=F32)

        kc(k).start()

    def along_x(k):
        kc(k).wait_recv()
        base = zfrom(k) * tokens

        @pl.loop(0, n_chunk)
        def _(r):
            rows = pl.ds(pl.multiple_of(r * CHUNK, CHUNK), CHUNK)
            mine = pl.ds(pl.multiple_of(base + r * CHUNK, CHUNK), CHUNK)
            xsend[k, rows, :] = (
                pown[k, 1 - x, rows, :] + precv[k, 1 - x, rows, :].astype(F32)
            ).astype(BF16)
            keys[mine, :] = pown[k, x, rows, :] + precv[k, x, rows, :].astype(F32)

        kx(k).start()

    def along_x_done(k):
        kx(k).wait_recv()
        base = zfrom(k) * tokens

        @pl.loop(0, n_chunk)
        def _(r):
            rows = pl.ds(pl.multiple_of(r * CHUNK, CHUNK), CHUNK)
            mine = pl.ds(pl.multiple_of(base + r * CHUNK, CHUNK), CHUNK)
            keysb[mine, :] = (keys[mine, :] + xrecv[k, rows, :].astype(F32)).astype(BF16)

    def relay(k):
        gz_arrived(k).wait_recv()
        gx(k).start()
        gc(k).start()

    project(0)

    row_ids = lax.broadcasted_iota(jnp.int32, (32, N_DP * tokens), 0)

    @pl.loop(0, N_DP * tokens // 32)
    def _(r):
        rows = pl.ds(pl.multiple_of(r * 32, 32), 32)
        order[rows, :] = jnp.where(dest_ref[...] == row_ids + r * 32, 1.0, 0.0).astype(BF16)

    along_x(0)
    for k in range(1, N_DP):
        relay(k)
        project(k)
        along_x(k)
        along_x_done(k - 1)
        gx_arrived(k - 1).wait_recv()
        gxc(k - 1).start()
    along_x_done(N_DP - 1)

    def kz(k):
        return send(ksend.at[k], krecv.at[k - 1], kz_ss.at[k - 1], kz_rs.at[k - 1], {"dp": zto(k)})

    for k in (1, 2, 3, 0):
        owner = pl.ds(pl.multiple_of(zto(k) * tokens, tokens), tokens)
        ksend[k] = jnp.dot(order[owner, :], keysb[...], preferred_element_type=F32).astype(BF16)
        if k:
            kz(k).start()
    gx_arrived(N_DP - 1).wait_recv()
    gxc(N_DP - 1).start()

    @pl.loop(0, 2 * N_DP)
    def _(b):
        rows = pl.ds(pl.multiple_of(b * (tokens // 2), tokens // 2), tokens // 2)
        jown[rows, :] = jnp.dot(
            order[rows, :], jfeat[...], preferred_element_type=F32
        ).astype(BF16)

    @pl.loop(0, N_DP * n_chunk)
    def _(b):
        block = pl.ds(pl.multiple_of(b * CHUNK, CHUNK), CHUNK)
        jturn[:, block] = jown[block, :].T

    for k in range(N_DP):
        gc_arrived(k, t_c).wait_recv()
        gc_arrived(4 + k, t_xc).wait_recv()
    for n in range(N_TP):
        cols = pl.ds(n * share, share)

        @pl.loop(0, feats // CHUNK)
        def _(r, cols=cols):
            rows = pl.ds(pl.multiple_of(r * CHUNK, CHUNK), CHUNK)
            value = jnp.zeros((CHUNK, share), F32)
            for d in range(N_DP):
                value = value + jnp.dot(
                    jturn[rows, pl.ds(d * tokens, tokens)],
                    gbuf[d, :, cols],
                    preferred_element_type=F32,
                )
            wgrad_ref[rows, cols] = value

    for k in range(1, N_DP):
        kz(k).wait_recv()
    decay = decay_ref[...]
    at_start = lax.broadcasted_iota(jnp.int32, (CHUNK, share), 0) % SEG == 0

    def down(values):
        return jnp.where(at_start, 0.0, pltpu.roll(values, 1, 0))

    @pl.loop(0, n_chunk)
    def _(r):
        rows = pl.ds(pl.multiple_of(r * CHUNK, CHUNK), CHUNK)
        value = ksend[0, rows, :].astype(F32)
        for k in range(1, N_DP):
            value = value + krecv[k - 1, rows, :].astype(F32)
        second = value + decay * down(value)
        third = value + decay * down(second)
        states_ref[0, rows, :] = value.astype(BF16)
        states_ref[1, rows, :] = second.astype(BF16)
        states_ref[2, rows, :] = third.astype(BF16)

    for k in range(1, N_DP):
        gz(k).wait_send()
        sq(k).wait_send()
        kz(k).wait_send()
        for i in range(n_chunk):
            jsend(k, i).wait_send()
    for k in range(N_DP):
        gx(k).wait_send()
        gc(k).wait_send()
        gxc(k).wait_send()
        kc(k).wait_send()
        kx(k).wait_send()


def fused(
    hidden_rows,
    layer_gain,
    key_weight,
    step_decay,
    owner_list,
    segment_len,
    reweight_count,
    loss_mask,
    state_cotangent,
):
    dp_index = lax.axis_index("dp")
    seg_count = N_DP * SEG_DEV
    share = state_cotangent.shape[3]
    tokens, layers, width = hidden_rows.shape
    feats, key_width = key_weight.shape
    ids = jnp.arange(seg_count)
    same = owner_list[None, :] == owner_list[:, None]
    rank = jnp.sum(same & (ids[None, :] < ids[:, None]), axis=1)
    destination = owner_list * SEG_DEV + rank
    source_of = jnp.sum(jnp.where(destination[None, :] == ids[:, None], ids[None, :], 0), axis=1)
    my_source = lax.dynamic_slice_in_dim(source_of, dp_index * SEG_DEV, SEG_DEV, 0)

    mask_table = loss_mask.reshape(seg_count, SEG).astype(F32)
    scale_table = mask_table * reweight_count.astype(F32)[:, None]
    pick = (my_source[:, None] == ids[None, :]).astype(F32)
    scale_owner = jnp.sum(pick[:, :, None] * scale_table[None], axis=1)
    state_grads = state_cotangent.astype(F32) * scale_owner[None, :, :, None]
    key_grads = unrolled_grads(state_grads, step_decay).astype(BF16)
    key_grads = key_grads.reshape(tokens, share)
    my_len = lax.dynamic_slice_in_dim(segment_len, dp_index * SEG_DEV, SEG_DEV, 0)
    live = (jnp.arange(SEG)[None, :] < my_len[:, None]).astype(F32).reshape(1, tokens)

    dest_rows = (destination[:, None] * SEG + jnp.arange(SEG)[None, :]).reshape(1, -1)

    vmem = pl.BlockSpec(memory_space=pltpu.VMEM)
    dma = pltpu.SemaphoreType.DMA
    n_chunk = tokens // CHUNK
    states, weight_grad = pl.pallas_call(
        fused_kernel,
        out_shape=(
            jax.ShapeDtypeStruct((3, tokens, share), BF16),
            jax.ShapeDtypeStruct((feats, key_width), F32),
        ),
        in_specs=[
            vmem,
            pl.BlockSpec(memory_space=pl.ANY),
            vmem,
            vmem,
            vmem,
            vmem,
            vmem,
        ],
        out_specs=(vmem, vmem),
        scratch_shapes=[
            pltpu.VMEM((layers, tokens, width), BF16),
            pltpu.VMEM((tokens, 128), F32),
            pltpu.VMEM((8, tokens), F32),
            pltpu.VMEM((3, 8, tokens), F32),
            pltpu.VMEM((tokens, 128), F32),
            pltpu.VMEM((3, tokens, feats), BF16),
            pltpu.VMEM((N_DP * tokens, feats), BF16),
            pltpu.VMEM((N_DP * tokens, feats), BF16),
            pltpu.VMEM((feats, N_DP * tokens), BF16),
            pltpu.VMEM((N_DP * tokens, N_DP * tokens), BF16),
            pltpu.VMEM((N_DP, tokens, key_width), BF16),
            pltpu.VMEM((N_DP, 2, tokens, share), BF16),
            pltpu.VMEM((N_DP, 2, tokens, share), BF16),
            pltpu.VMEM((N_DP, 2, tokens, share), F32),
            pltpu.VMEM((N_DP, tokens, share), BF16),
            pltpu.VMEM((N_DP, tokens, share), BF16),
            pltpu.VMEM((N_DP * tokens, share), F32),
            pltpu.VMEM((N_DP * tokens, share), BF16),
            pltpu.VMEM((N_DP, tokens, share), BF16),
            pltpu.VMEM((N_DP - 1, tokens, share), BF16),
            dma((n_chunk,)),
            dma((3,)),
            dma((3,)),
            dma((3, n_chunk)),
            dma((3, n_chunk)),
            dma((3,)),
            dma((3,)),
            dma((4,)),
            dma((4,)),
            dma((8,)),
            dma((8,)),
            dma((4,)),
            dma((4,)),
            dma((4,)),
            dma((4,)),
            dma((3,)),
            dma((3,)),
        ],
        compiler_params=pltpu.CompilerParams(
            collective_id=0, has_side_effects=True, vmem_limit_bytes=56 * 1024 * 1024
        ),
        cost_estimate=pl.CostEstimate(
            flops=4 * N_DP * tokens * feats * key_width,
            bytes_accessed=12 * 1024 * 1024,
            transcendentals=0,
        ),
        name="draft_head",
    )(
        dest_rows.astype(jnp.int32),
        hidden_rows.transpose(1, 0, 2),
        layer_gain,
        live,
        key_weight,
        step_decay.reshape(1, share),
        key_grads,
    )
    return (states.reshape(3, SEG_DEV, SEG, share), weight_grad)


def uses_kernel(mesh):
    return mesh.shape["dp"] == N_DP and mesh.shape["tensor"] == N_TP


def solution(mesh):
    return jax.shard_map(
        fused if uses_kernel(mesh) else per_device,
        mesh=mesh,
        in_specs=(
            P(("groups", "dp"), None, "tensor"),
            P(None, "tensor"),
            P(("tensor", "dp"), None),
            P("tensor"),
            P("groups"),
            P("groups"),
            P("groups"),
            P("groups"),
            P(None, ("groups", "dp"), None, "tensor"),
        ),
        out_specs=(P(None, ("groups", "dp"), None, "tensor"), P(("groups", "tensor", "dp"), None)),
        check_vma=False,
    )
```

```python
import jax
import jax.numpy as jnp
from jax import lax
from jax.experimental import pallas as pl
from jax.experimental.pallas import tpu as pltpu
from jax.sharding import PartitionSpec as P

D = 8192
SEG = 16
SEG_DEV = 32


epsilon = 1e-05


def shift_down(values):
    zeros = jnp.zeros_like(values[:, :1])
    return jnp.concatenate([zeros, values[:, :-1]], axis=1)


def shift_up(values):
    zeros = jnp.zeros_like(values[:, :1])
    return jnp.concatenate([values[:, 1:], zeros], axis=1)


def unrolled_steps(key_rows, decay_part):
    second = key_rows + decay_part * shift_down(key_rows)
    third = key_rows + decay_part * shift_down(second)
    return jnp.stack([key_rows, second, third])


def unrolled_grads(state_grads, decay_part):
    grad_third = state_grads[2]
    grad_second = state_grads[1] + decay_part * shift_up(grad_third)
    grad_first = state_grads[0] + decay_part * shift_up(grad_second)
    return grad_first + grad_second + grad_third


def layer_squares(row_block):
    values = row_block.astype(jnp.float32)
    return jnp.sum(values * values, axis=-1)


def normalize(row_block, squares, live_mask, layer_gain):
    inverse = lax.rsqrt(squares / D + epsilon)
    mixture = jnp.sum(row_block.astype(jnp.float32) * layer_gain * inverse[..., None], axis=2)
    return (mixture * live_mask[..., None]).astype(jnp.bfloat16)


def per_device(
    hidden_rows,
    layer_gain,
    key_weight,
    step_decay,
    owner_list,
    segment_len,
    reweight_count,
    loss_mask,
    state_cotangent,
):
    dp_count = lax.axis_size("dp")
    dp_index = lax.axis_index("dp")
    tp_index = lax.axis_index("tensor")
    part_width = hidden_rows.shape[2]
    key_width = key_weight.shape[1]
    share_width = state_cotangent.shape[3]
    capacity = max(2, (2 * SEG_DEV + dp_count - 1) // dp_count)
    slot_total = dp_count * capacity
    owner_table = owner_list.reshape(dp_count, SEG_DEV)
    positions = jnp.arange(SEG)
    segment_ids = jnp.arange(dp_count * SEG_DEV)
    local_ids = jnp.arange(SEG_DEV)
    slot_ids = jnp.arange(slot_total)
    zero_value = jnp.zeros((), jnp.bfloat16)
    my_owners = lax.dynamic_index_in_dim(owner_table, dp_index, 0, keepdims=False)
    earlier = (my_owners[None, :] == my_owners[:, None]) & (local_ids[None, :] < local_ids[:, None])
    slot_out = my_owners * capacity + jnp.sum(earlier, axis=1)
    out_match = slot_ids[:, None] == slot_out[None, :]
    send_pick = jnp.sum(jnp.where(out_match, local_ids[None, :], 0), axis=1)
    send_used = jnp.any(out_match, axis=1)
    incoming = owner_table == dp_index
    flat_in = incoming.reshape(-1)
    rank_flat = jnp.cumsum(flat_in.astype(jnp.int32)) - 1
    within_src = (jnp.cumsum(incoming.astype(jnp.int32), axis=1) - 1).reshape(-1)
    chosen = (rank_flat[None, :] == local_ids[:, None]) & flat_in[None, :]
    global_seg = jnp.sum(jnp.where(chosen, segment_ids[None, :], 0), axis=1)
    slot_in = jnp.sum(
        jnp.where(chosen, (segment_ids // SEG_DEV * capacity + within_src)[None, :], 0), axis=1
    )
    live_owner = (positions[None, :] < segment_len[global_seg][:, None]).astype(jnp.float32)
    mask_table = loss_mask.reshape(dp_count * SEG_DEV, SEG).astype(jnp.float32)
    weight_table = reweight_count.astype(jnp.float32)
    scale_owner = mask_table[global_seg] * weight_table[global_seg][:, None]
    row_block = hidden_rows.reshape(SEG_DEV, SEG, hidden_rows.shape[1], part_width)
    outgoing = jnp.where(send_used[:, None, None, None], row_block[send_pick], zero_value)
    arrived = lax.all_to_all(outgoing, "dp", split_axis=0, concat_axis=0, tiled=True)
    owner_rows = arrived[slot_in]
    squares = lax.psum(layer_squares(owner_rows), "tensor")
    joined_rows = normalize(owner_rows, squares, live_owner, layer_gain)
    flat_rows = joined_rows.reshape(-1, part_width)
    columns = flat_rows
    partial_keys = jnp.dot(
        columns,
        lax.all_gather(key_weight, "dp", axis=0, tiled=True),
        preferred_element_type=jnp.float32,
    )
    summed_keys = lax.psum(partial_keys, "tensor")
    key_share = lax.dynamic_slice_in_dim(summed_keys, tp_index * share_width, share_width, 1)
    states = unrolled_steps(key_share.reshape(SEG_DEV, SEG, share_width), step_decay).astype(
        jnp.bfloat16
    )
    state_grads = state_cotangent.astype(jnp.float32) * scale_owner[None, :, :, None]
    key_grads = unrolled_grads(state_grads, step_decay).astype(jnp.bfloat16)
    all_grads = lax.all_gather(key_grads, "tensor", axis=2, tiled=True)
    flat_grads = all_grads.reshape(-1, key_width)
    weight_flat_rows = joined_rows.reshape(-1, part_width)
    columns = weight_flat_rows
    weight_grad = lax.psum_scatter(
        lax.dot_general(
            columns, flat_grads, (((0,), (0,)), ((), ())), preferred_element_type=jnp.float32
        ),
        "dp",
        scatter_dimension=0,
        tiled=True,
    )
    return (states, weight_grad)


N_DP = 4
N_TP = 4
CHUNK = 128
BF16 = jnp.bfloat16
F32 = jnp.float32


def fused_kernel(
    owner_ref,
    length_ref,
    count_ref,
    mask_ref,
    hidden_ref,
    gain_ref,
    weight_ref,
    decay_ref,
    cotangent_ref,
    states_ref,
    wgrad_ref,
    hid,
    dest,
    grads,
    sqcol,
    sqsend,
    sqrecv,
    invcol,
    jloc,
    jfeat,
    jown,
    jturn,
    order,
    gbuf,
    psend,
    precv,
    pown,
    xsend,
    xrecv,
    keys,
    keysb,
    kpart,
    ksend,
    krecv,
    hid_sem,
    sq_ss,
    sq_rs,
    j_ss,
    j_rs,
    gz_ss,
    gz_rs,
    gx_ss,
    gx_rs,
    gc_ss,
    gc_rs,
    kc_ss,
    kc_rs,
    kx_ss,
    kx_rs,
    kz_ss,
    kz_rs,
):
    z = lax.axis_index("dp")
    t = lax.axis_index("tensor")
    x = t // 2
    c = t % 2
    t_x = (t + 2) % N_TP
    t_c = t + 1 - 2 * c
    t_xc = (t_c + 2) % N_TP
    tokens = hid.shape[1]
    feats = weight_ref.shape[0]
    share = grads.shape[1]
    n_chunk = tokens // CHUNK

    def zto(k):
        return (z + k) % N_DP

    def zfrom(k):
        return (z + N_DP - k) % N_DP

    def lanes(index, width):
        return pl.ds(pl.multiple_of(index * width, width), width)

    def send(src, dst, ss, rs, where):
        return pltpu.make_async_remote_copy(
            src_ref=src,
            dst_ref=dst,
            send_sem=ss,
            recv_sem=rs,
            device_id=where,
            device_id_type=pl.DeviceIdType.MESH,
        )

    def hid_copy(i):
        rows = pl.ds(i * CHUNK, CHUNK)
        return pltpu.make_async_copy(hidden_ref.at[:, rows], hid.at[:, rows], hid_sem.at[i])

    for i in range(n_chunk):
        hid_copy(i).start()

    barrier = pltpu.get_barrier_semaphore()
    for k in range(1, N_DP):
        pl.semaphore_signal(
            barrier, inc=1, device_id={"dp": zto(k)}, device_id_type=pl.DeviceIdType.MESH
        )
    for k in range(1, N_TP):
        pl.semaphore_signal(
            barrier,
            inc=1,
            device_id={"tensor": (t + k) % N_TP},
            device_id_type=pl.DeviceIdType.MESH,
        )
    pl.semaphore_wait(barrier, N_DP + N_TP - 2)

    seg_count = N_DP * SEG_DEV
    all_tokens = N_DP * tokens
    square = (seg_count, seg_count)
    owner_row = owner_ref[...].astype(F32)
    across = jnp.broadcast_to(owner_row, square)
    earlier = lax.broadcasted_iota(jnp.int32, square, 0) < lax.broadcasted_iota(
        jnp.int32, square, 1
    )
    match = jnp.where(earlier, jnp.where(across == across.T, 1.0, 0.0), 0.0)
    dest_seg = owner_row * SEG_DEV + jnp.sum(match, axis=0, keepdims=True)
    sub = lax.broadcasted_iota(jnp.int32, (8, seg_count), 0)
    rows8 = jnp.where(
        sub == 0,
        dest_seg,
        jnp.where(sub == 1, count_ref[...].astype(F32), length_ref[...].astype(F32)),
    ).astype(BF16)

    def spread(first, width):
        shape = (seg_count, width)
        token_seg = lax.broadcasted_iota(jnp.int32, shape, 1) // SEG + first
        hot = jnp.where(lax.broadcasted_iota(jnp.int32, shape, 0) == token_seg, 1.0, 0.0)
        return jnp.dot(rows8, hot.astype(BF16), preferred_element_type=F32)

    whole = spread(0, all_tokens)
    place = (lax.broadcasted_iota(jnp.int32, (1, all_tokens), 1) % SEG).astype(F32)
    dest[...] = whole[0:1] * SEG + place
    scale_row = whole[1:2] * mask_ref[...].astype(F32)
    scale_rows = jnp.broadcast_to(scale_row, (128, all_tokens)).astype(BF16)
    here = spread(z * SEG_DEV, tokens)
    live = jnp.where(place[:, :tokens] < here[2:3], 1.0, 0.0)

    def fill_order(first, count):
        @pl.loop(0, count // 16)
        def _(r):
            start = pl.multiple_of(first + r * 16, 16)
            ids = lax.broadcasted_iota(jnp.int32, (16, all_tokens), 0) + start
            order[pl.ds(start, 16), :] = jnp.where(dest[...] == ids.astype(F32), 1.0, 0.0).astype(
                BF16
            )

    fill_order(z * tokens, tokens)

    decay = decay_ref[...]
    positions = lax.broadcasted_iota(jnp.int32, (CHUNK, share), 0) % SEG

    def down(values):
        return jnp.where(positions == 0, 0.0, pltpu.roll(values, 1, 0))

    def up(values):
        return jnp.where(positions == SEG - 1, 0.0, pltpu.roll(values, CHUNK - 1, 0))

    for r in range(n_chunk):
        rows = pl.ds(r * CHUNK, CHUNK)
        mine = pl.ds(pl.multiple_of(z * tokens + r * CHUNK, CHUNK), CHUNK)
        scale = lax.dot_general(
            order[mine, :], scale_rows, (((1,), (1,)), ((), ())), preferred_element_type=F32
        )
        scale = jnp.concatenate([scale] * (share // 128), axis=1)
        third = cotangent_ref[2, rows, :].astype(F32) * scale
        second = cotangent_ref[1, rows, :].astype(F32) * scale + decay * up(third)
        first = cotangent_ref[0, rows, :].astype(F32) * scale + decay * up(second)
        total = (first + second + third).astype(BF16)
        grads[rows, :] = total
        gbuf[z, rows, lanes(t, share)] = total

    def g_block(zi, ti):
        return gbuf.at[zi, :, lanes(ti, share)]

    def gz(side, hop):
        step = 1 - 2 * side
        src = z - step * hop
        block = g_block(src, t)
        return send(
            grads if hop == 0 else block,
            block,
            gz_ss.at[side, hop],
            gz_rs.at[side, hop],
            {"dp": z + step},
        )

    def gx(d):
        block = g_block(d, t)
        return send(block, block, gx_ss.at[d], gx_rs.at[d], {"tensor": t_x})

    def gc(d):
        block = g_block(d, t)
        return send(block, block, gc_ss.at[d], gc_rs.at[d], {"tensor": t_c})

    def gxc(d):
        block = g_block(d, t_x)
        return send(block, block, gc_ss.at[4 + d], gc_rs.at[4 + d], {"tensor": t_c})

    def gz_arrived(side, hop):
        step = 1 - 2 * side
        block = g_block(z - step * hop, t)
        return send(
            block, block, gz_ss.at[side, hop - 1], gz_rs.at[side, hop - 1], {"dp": z - step}
        )

    def gx_arrived(d):
        block = g_block(d, t_x)
        return send(block, block, gx_ss.at[d], gx_rs.at[d], {"tensor": t_x})

    def gc_arrived(k, ti):
        block = g_block(k % 4, ti)
        return send(block, block, gc_ss.at[k], gc_rs.at[k], {"tensor": t_c})

    def came(side, hop):
        return z >= hop if side == 0 else z + hop < N_DP

    def goes(side, hop):
        return came(side, hop) & (z < N_DP - 1 if side == 0 else z > 0)

    def pass_on(hop):
        for side in range(2):

            @pl.when(goes(side, hop))
            def _(side=side):
                gz(side, hop).start()

    pass_on(0)
    gx(z).start()
    gc(z).start()

    def relay(hop):
        for side in range(2):

            @pl.when(came(side, hop))
            def _(side=side):
                gz_arrived(side, hop).wait_recv()

        if hop < N_DP - 1:
            pass_on(hop)
        for side in range(2):

            @pl.when(came(side, hop))
            def _(side=side):
                src = z - (1 - 2 * side) * hop
                gx(src).start()
                gc(src).start()

    lane = lax.broadcasted_iota(jnp.int32, (32, 128), 1)
    for i in range(n_chunk):
        hid_copy(i).wait()

        @pl.loop(0, CHUNK // 32)
        def _(r, i=i):
            rows = pl.ds(pl.multiple_of(i * CHUNK + r * 32, 32), 32)
            sums = []
            for layer in range(3):
                values = hid[layer, rows, :].astype(F32)
                sums.append(jnp.sum(values * values, axis=-1, keepdims=True))
            sqcol[rows, :] = jnp.where(
                lane == 0, sums[0], jnp.where(lane == 1, sums[1], sums[2])
            )

    sqsend[...] = sqcol[...].T[:8]

    def sq(k):
        return send(
            sqsend,
            sqrecv.at[k - 1],
            sq_ss.at[k - 1],
            sq_rs.at[k - 1],
            {"tensor": (t + k) % N_TP},
        )

    for k in range(1, N_TP):
        sq(k).start()
    for k in range(1, N_TP):
        sq(k).wait_recv()
    total = sqsend[...] + sqrecv[0] + sqrecv[1] + sqrecv[2]
    inverse = lax.rsqrt(total / D + epsilon) * live
    invcol[...] = jnp.concatenate([inverse, jnp.zeros((120, tokens), F32)], axis=0).T

    def jsend(k, i):
        rows = pl.ds(i * CHUNK, CHUNK)
        return send(
            jloc.at[k - 1, rows],
            jfeat.at[pl.ds(pl.multiple_of(z * tokens + i * CHUNK, CHUNK), CHUNK)],
            j_ss.at[k - 1, i],
            j_rs.at[k - 1, i],
            {"dp": zto(k)},
        )

    def jarrived(k, i):
        rows = pl.ds(pl.multiple_of(zfrom(k) * tokens + i * CHUNK, CHUNK), CHUNK)
        return send(
            jfeat.at[rows], jfeat.at[rows], j_ss.at[k - 1, i], j_rs.at[k - 1, i], {"dp": zto(k)}
        )

    for i in range(n_chunk):
        for k in (1, 2, 3, 0):
            cols = lanes(zto(k), feats)

            @pl.loop(0, CHUNK // 16)
            def _(r, i=i, k=k, cols=cols):
                rows = pl.ds(pl.multiple_of(i * CHUNK + r * 16, 16), 16)
                factors = invcol[rows, :]
                mixture = jnp.zeros((16, feats), F32)
                for layer in range(3):
                    scaled = hid[layer, rows, cols].astype(F32) * gain_ref[pl.ds(layer, 1), cols]
                    mixture = mixture + scaled * factors[:, layer : layer + 1]
                if k:
                    jloc[k - 1, rows, :] = mixture.astype(BF16)
                else:
                    mine = pl.ds(pl.multiple_of(z * tokens + i * CHUNK + r * 16, 16), 16)
                    jfeat[mine, :] = mixture.astype(BF16)

            if k:
                jsend(k, i).start()
        if i:
            relay(i)

    n_unit = N_DP * n_chunk

    def unit_rows(u):
        far = jnp.where(u < n_chunk, 0, (u + 3 * N_DP - n_chunk) % (N_DP - 1) + 1)
        part = jnp.where(u < n_chunk, u, (u + 3 * N_DP - n_chunk) // (N_DP - 1) - N_DP)
        return far, part, pl.multiple_of(zfrom(far) * tokens + part * CHUNK, CHUNK)

    def kc(u):
        return send(psend.at[u], precv.at[u], kc_ss.at[u], kc_rs.at[u], {"tensor": t_c})

    def kx(u):
        return send(xsend.at[u], xrecv.at[u], kx_ss.at[u], kx_rs.at[u], {"tensor": t_x})

    def project(u):
        _, _, start = unit_rows(u)
        block = jfeat[pl.ds(start, CHUNK), :]
        for half in range(2):
            other = weight_ref[:, lanes(2 * half + 1 - c, share)]
            psend[u, half] = jnp.dot(block, other, preferred_element_type=F32).astype(BF16)
        kc(u).start()
        for half in range(2):
            own = weight_ref[:, lanes(2 * half + c, share)]
            pown[u, half] = jnp.dot(block, own, preferred_element_type=F32)

    def along_x(u):
        kc(u).wait_recv()
        _, _, start = unit_rows(u)
        xsend[u] = (pown[u, 1 - x] + precv[u, 1 - x].astype(F32)).astype(BF16)
        kx(u).start()
        keys[pl.ds(start, CHUNK), :] = pown[u, x] + precv[u, x].astype(F32)

    def along_x_done(u):
        kx(u).wait_recv()
        _, _, start = unit_rows(u)
        mine = pl.ds(start, CHUNK)
        keysb[mine, :] = (keys[mine, :] + xrecv[u].astype(F32)).astype(BF16)

    for k in range(1, N_DP):
        fill_order(zto(k) * tokens, tokens)

    @pl.loop(0, n_unit + 2)
    def _(step):
        @pl.when((step >= n_chunk) & (step < n_unit))
        def _():
            far, part, _ = unit_rows(step)
            jarrived(far, part).wait_recv()

        @pl.when(step < n_unit)
        def _():
            project(step)

        @pl.when((step >= 1) & (step <= n_unit))
        def _():
            along_x(step - 1)

        @pl.when(step >= 2)
        def _():
            along_x_done(step - 2)

    def kz(side, o):
        return send(
            ksend.at[o],
            krecv.at[side, o],
            kz_ss.at[side, o],
            kz_rs.at[side, o],
            {"dp": z + 1 - 2 * side},
        )

    def kz_arrived(side, o):
        return send(
            ksend.at[o],
            krecv.at[side, o],
            kz_ss.at[side, o],
            kz_rs.at[side, o],
            {"dp": z - 1 + 2 * side},
        )

    def own_part(o):
        return jnp.dot(
            order[o * tokens : (o + 1) * tokens, :], keysb[...], preferred_element_type=F32
        )

    last = N_DP - 1

    @pl.when(z == 0)
    def _():
        for o in (3, 2, 1):
            ksend[o] = own_part(o).astype(BF16)
            kz(0, o).start()
        kpart[0] = own_part(0)

    @pl.when(z == last)
    def _():
        for o in (0, 1, 2):
            ksend[o] = own_part(o).astype(BF16)
            kz(1, o).start()
        kpart[3] = own_part(3)

    @pl.when((z > 0) & (z < last))
    def _():
        for o in range(N_DP):
            kpart[o] = own_part(o)

    def stage(j):
        for side, o in ((0, last - j), (1, j)):

            @pl.when((z > 0) & (z < last) & (z < o if side == 0 else z > o))
            def _(side=side, o=o):
                kz_arrived(side, o).wait_recv()
                ksend[o] = (kpart[o] + krecv[side, o].astype(F32)).astype(BF16)
                kz(side, o).start()

    for d in range(N_DP):
        gx_arrived(d).wait_recv()
        gxc(d).start()

    @pl.loop(0, 2 * N_DP)
    def _(b):
        rows = pl.ds(pl.multiple_of(b * (tokens // 2), tokens // 2), tokens // 2)
        jown[rows, :] = jnp.dot(
            order[rows, :], jfeat[...], preferred_element_type=F32
        ).astype(BF16)

    @pl.loop(0, N_DP * n_chunk)
    def _(b):
        block = pl.ds(pl.multiple_of(b * CHUNK, CHUNK), CHUNK)
        jturn[:, block] = jown[block, :].T

    stage(0)
    for k in range(N_DP):
        gc_arrived(k, t_c).wait_recv()
        gc_arrived(4 + k, t_xc).wait_recv()
    for n in range(N_TP):
        if n == 2:
            stage(1)
        cols = pl.ds(n * share, share)

        @pl.loop(0, feats // CHUNK)
        def _(r, cols=cols):
            rows = pl.ds(pl.multiple_of(r * CHUNK, CHUNK), CHUNK)
            value = jnp.zeros((CHUNK, share), F32)
            for d in range(N_DP):
                value = value + jnp.dot(
                    jturn[rows, pl.ds(d * tokens, tokens)],
                    gbuf[d, :, cols],
                    preferred_element_type=F32,
                )
            wgrad_ref[rows, cols] = value

    stage(2)

    @pl.when(z > 0)
    def _():
        kz_arrived(0, z).wait_recv()
        kpart[z] = kpart[z] + krecv[0, z].astype(F32)

    @pl.when(z < last)
    def _():
        kz_arrived(1, z).wait_recv()
        kpart[z] = kpart[z] + krecv[1, z].astype(F32)

    @pl.loop(0, n_chunk)
    def _(r):
        rows = pl.ds(pl.multiple_of(r * CHUNK, CHUNK), CHUNK)
        value = kpart[z, rows, :]
        second = value + decay * down(value)
        third = value + decay * down(second)
        states_ref[0, rows, :] = value.astype(BF16)
        states_ref[1, rows, :] = second.astype(BF16)
        states_ref[2, rows, :] = third.astype(BF16)

    for k in range(1, N_DP):
        sq(k).wait_send()
        for i in range(n_chunk):
            jsend(k, i).wait_send()
    for hop in range(N_DP - 1):
        for side in range(2):

            @pl.when(goes(side, hop))
            def _(side=side, hop=hop):
                gz(side, hop).wait_send()

    for d in range(N_DP):
        gx(d).wait_send()
        gc(d).wait_send()
        gxc(d).wait_send()

        @pl.when(z < d)
        def _(d=d):
            kz(0, d).wait_send()

        @pl.when(z > d)
        def _(d=d):
            kz(1, d).wait_send()

    @pl.loop(0, n_unit)
    def _(u):
        kc(u).wait_send()
        kx(u).wait_send()


def fused(
    hidden_rows,
    layer_gain,
    key_weight,
    step_decay,
    owner_list,
    segment_len,
    reweight_count,
    loss_mask,
    state_cotangent,
):
    share = state_cotangent.shape[3]
    tokens, layers, width = hidden_rows.shape
    feats, key_width = key_weight.shape

    vmem = pl.BlockSpec(memory_space=pltpu.VMEM)
    dma = pltpu.SemaphoreType.DMA
    n_chunk = tokens // CHUNK
    n_unit = N_DP * n_chunk
    states, weight_grad = pl.pallas_call(
        fused_kernel,
        out_shape=(
            jax.ShapeDtypeStruct((3, tokens, share), BF16),
            jax.ShapeDtypeStruct((feats, key_width), F32),
        ),
        in_specs=[
            vmem,
            vmem,
            vmem,
            vmem,
            pl.BlockSpec(memory_space=pl.ANY),
            vmem,
            vmem,
            vmem,
            vmem,
        ],
        out_specs=(vmem, vmem),
        scratch_shapes=[
            pltpu.VMEM((layers, tokens, width), BF16),
            pltpu.VMEM((1, N_DP * tokens), F32),
            pltpu.VMEM((tokens, share), BF16),
            pltpu.VMEM((tokens, 128), F32),
            pltpu.VMEM((8, tokens), F32),
            pltpu.VMEM((3, 8, tokens), F32),
            pltpu.VMEM((tokens, 128), F32),
            pltpu.VMEM((3, tokens, feats), BF16),
            pltpu.VMEM((N_DP * tokens, feats), BF16),
            pltpu.VMEM((N_DP * tokens, feats), BF16),
            pltpu.VMEM((feats, N_DP * tokens), BF16),
            pltpu.VMEM((N_DP * tokens, N_DP * tokens), BF16),
            pltpu.VMEM((N_DP, tokens, key_width), BF16),
            pltpu.VMEM((n_unit, 2, CHUNK, share), BF16),
            pltpu.VMEM((n_unit, 2, CHUNK, share), BF16),
            pltpu.VMEM((n_unit, 2, CHUNK, share), F32),
            pltpu.VMEM((n_unit, CHUNK, share), BF16),
            pltpu.VMEM((n_unit, CHUNK, share), BF16),
            pltpu.VMEM((N_DP * tokens, share), F32),
            pltpu.VMEM((N_DP * tokens, share), BF16),
            pltpu.VMEM((N_DP, tokens, share), F32),
            pltpu.VMEM((N_DP, tokens, share), BF16),
            pltpu.VMEM((2, N_DP, tokens, share), BF16),
            dma((n_chunk,)),
            dma((3,)),
            dma((3,)),
            dma((3, n_chunk)),
            dma((3, n_chunk)),
            dma((2, 3)),
            dma((2, 3)),
            dma((4,)),
            dma((4,)),
            dma((8,)),
            dma((8,)),
            dma((n_unit,)),
            dma((n_unit,)),
            dma((n_unit,)),
            dma((n_unit,)),
            dma((2, 4)),
            dma((2, 4)),
        ],
        compiler_params=pltpu.CompilerParams(
            collective_id=0, has_side_effects=True, vmem_limit_bytes=60 * 1024 * 1024
        ),
        cost_estimate=pl.CostEstimate(
            flops=4 * N_DP * tokens * feats * key_width,
            bytes_accessed=12 * 1024 * 1024,
            transcendentals=0,
        ),
        name="draft_head",
    )(
        owner_list.reshape(1, -1),
        segment_len.reshape(1, -1),
        reweight_count.reshape(1, -1),
        loss_mask.reshape(1, -1),
        hidden_rows.transpose(1, 0, 2),
        layer_gain,
        key_weight,
        step_decay.reshape(1, share),
        state_cotangent.reshape(3, tokens, share),
    )
    return (states.reshape(3, SEG_DEV, SEG, share), weight_grad)


def uses_kernel(mesh):
    return mesh.shape["dp"] == N_DP and mesh.shape["tensor"] == N_TP


def solution(mesh):
    return jax.shard_map(
        fused if uses_kernel(mesh) else per_device,
        mesh=mesh,
        in_specs=(
            P(("groups", "dp"), None, "tensor"),
            P(None, "tensor"),
            P(("tensor", "dp"), None),
            P("tensor"),
            P("groups"),
            P("groups"),
            P("groups"),
            P("groups"),
            P(None, ("groups", "dp"), None, "tensor"),
        ),
        out_specs=(P(None, ("groups", "dp"), None, "tensor"), P(("groups", "tensor", "dp"), None)),
        check_vma=False,
    )
```

```python
import jax
import jax.numpy as jnp
from jax import lax
from jax.experimental import pallas as pl
from jax.experimental.pallas import tpu as pltpu
from jax.sharding import PartitionSpec as P

D = 8192
SEG = 16
SEG_DEV = 32


epsilon = 1e-05


def shift_down(values):
    zeros = jnp.zeros_like(values[:, :1])
    return jnp.concatenate([zeros, values[:, :-1]], axis=1)


def shift_up(values):
    zeros = jnp.zeros_like(values[:, :1])
    return jnp.concatenate([values[:, 1:], zeros], axis=1)


def unrolled_steps(key_rows, decay_part):
    second = key_rows + decay_part * shift_down(key_rows)
    third = key_rows + decay_part * shift_down(second)
    return jnp.stack([key_rows, second, third])


def unrolled_grads(state_grads, decay_part):
    grad_third = state_grads[2]
    grad_second = state_grads[1] + decay_part * shift_up(grad_third)
    grad_first = state_grads[0] + decay_part * shift_up(grad_second)
    return grad_first + grad_second + grad_third


def layer_squares(row_block):
    values = row_block.astype(jnp.float32)
    return jnp.sum(values * values, axis=-1)


def normalize(row_block, squares, live_mask, layer_gain):
    inverse = lax.rsqrt(squares / D + epsilon)
    mixture = jnp.sum(row_block.astype(jnp.float32) * layer_gain * inverse[..., None], axis=2)
    return (mixture * live_mask[..., None]).astype(jnp.bfloat16)


def per_device(
    hidden_rows,
    layer_gain,
    key_weight,
    step_decay,
    owner_list,
    segment_len,
    reweight_count,
    loss_mask,
    state_cotangent,
):
    dp_count = lax.axis_size("dp")
    dp_index = lax.axis_index("dp")
    tp_index = lax.axis_index("tensor")
    part_width = hidden_rows.shape[2]
    key_width = key_weight.shape[1]
    share_width = state_cotangent.shape[3]
    capacity = max(2, (2 * SEG_DEV + dp_count - 1) // dp_count)
    slot_total = dp_count * capacity
    owner_table = owner_list.reshape(dp_count, SEG_DEV)
    positions = jnp.arange(SEG)
    segment_ids = jnp.arange(dp_count * SEG_DEV)
    local_ids = jnp.arange(SEG_DEV)
    slot_ids = jnp.arange(slot_total)
    zero_value = jnp.zeros((), jnp.bfloat16)
    my_owners = lax.dynamic_index_in_dim(owner_table, dp_index, 0, keepdims=False)
    earlier = (my_owners[None, :] == my_owners[:, None]) & (local_ids[None, :] < local_ids[:, None])
    slot_out = my_owners * capacity + jnp.sum(earlier, axis=1)
    out_match = slot_ids[:, None] == slot_out[None, :]
    send_pick = jnp.sum(jnp.where(out_match, local_ids[None, :], 0), axis=1)
    send_used = jnp.any(out_match, axis=1)
    incoming = owner_table == dp_index
    flat_in = incoming.reshape(-1)
    rank_flat = jnp.cumsum(flat_in.astype(jnp.int32)) - 1
    within_src = (jnp.cumsum(incoming.astype(jnp.int32), axis=1) - 1).reshape(-1)
    chosen = (rank_flat[None, :] == local_ids[:, None]) & flat_in[None, :]
    global_seg = jnp.sum(jnp.where(chosen, segment_ids[None, :], 0), axis=1)
    slot_in = jnp.sum(
        jnp.where(chosen, (segment_ids // SEG_DEV * capacity + within_src)[None, :], 0), axis=1
    )
    live_owner = (positions[None, :] < segment_len[global_seg][:, None]).astype(jnp.float32)
    mask_table = loss_mask.reshape(dp_count * SEG_DEV, SEG).astype(jnp.float32)
    weight_table = reweight_count.astype(jnp.float32)
    scale_owner = mask_table[global_seg] * weight_table[global_seg][:, None]
    row_block = hidden_rows.reshape(SEG_DEV, SEG, hidden_rows.shape[1], part_width)
    outgoing = jnp.where(send_used[:, None, None, None], row_block[send_pick], zero_value)
    arrived = lax.all_to_all(outgoing, "dp", split_axis=0, concat_axis=0, tiled=True)
    owner_rows = arrived[slot_in]
    squares = lax.psum(layer_squares(owner_rows), "tensor")
    joined_rows = normalize(owner_rows, squares, live_owner, layer_gain)
    flat_rows = joined_rows.reshape(-1, part_width)
    columns = flat_rows
    partial_keys = jnp.dot(
        columns,
        lax.all_gather(key_weight, "dp", axis=0, tiled=True),
        preferred_element_type=jnp.float32,
    )
    summed_keys = lax.psum(partial_keys, "tensor")
    key_share = lax.dynamic_slice_in_dim(summed_keys, tp_index * share_width, share_width, 1)
    states = unrolled_steps(key_share.reshape(SEG_DEV, SEG, share_width), step_decay).astype(
        jnp.bfloat16
    )
    state_grads = state_cotangent.astype(jnp.float32) * scale_owner[None, :, :, None]
    key_grads = unrolled_grads(state_grads, step_decay).astype(jnp.bfloat16)
    all_grads = lax.all_gather(key_grads, "tensor", axis=2, tiled=True)
    flat_grads = all_grads.reshape(-1, key_width)
    weight_flat_rows = joined_rows.reshape(-1, part_width)
    columns = weight_flat_rows
    weight_grad = lax.psum_scatter(
        lax.dot_general(
            columns, flat_grads, (((0,), (0,)), ((), ())), preferred_element_type=jnp.float32
        ),
        "dp",
        scatter_dimension=0,
        tiled=True,
    )
    return (states, weight_grad)


N_DP = 4
N_TP = 4
CHUNK = 128
BF16 = jnp.bfloat16
F32 = jnp.float32


def fused_kernel(
    owner_ref,
    length_ref,
    count_ref,
    mask_ref,
    hidden_ref,
    gain_ref,
    weight_ref,
    decay_ref,
    cotangent_ref,
    states_ref,
    wgrad_ref,
    hid,
    dest,
    grads,
    sqcol,
    sqsend,
    sqrecv,
    invcol,
    jloc,
    jfeat,
    jown,
    jturn,
    order,
    gbuf,
    psend,
    precv,
    pown,
    xsend,
    xrecv,
    keys,
    keysb,
    kpart,
    ksend,
    krecv,
    hid_sem,
    sq_ss,
    sq_rs,
    j_ss,
    j_rs,
    gz_ss,
    gz_rs,
    gx_ss,
    gx_rs,
    gc_ss,
    gc_rs,
    kc_ss,
    kc_rs,
    kx_ss,
    kx_rs,
    kz_ss,
    kz_rs,
):
    z = lax.axis_index("dp")
    t = lax.axis_index("tensor")
    x = t // 2
    c = t % 2
    t_x = (t + 2) % N_TP
    t_c = t + 1 - 2 * c
    t_xc = (t_c + 2) % N_TP
    tokens = hid.shape[1]
    feats = weight_ref.shape[0]
    share = grads.shape[1]
    n_chunk = tokens // CHUNK

    def zto(k):
        return (z + k) % N_DP

    def zfrom(k):
        return (z + N_DP - k) % N_DP

    def lanes(index, width):
        return pl.ds(pl.multiple_of(index * width, width), width)

    def send(src, dst, ss, rs, where):
        return pltpu.make_async_remote_copy(
            src_ref=src,
            dst_ref=dst,
            send_sem=ss,
            recv_sem=rs,
            device_id=where,
            device_id_type=pl.DeviceIdType.MESH,
        )

    def hid_copy(i):
        rows = pl.ds(i * CHUNK, CHUNK)
        return pltpu.make_async_copy(hidden_ref.at[:, rows], hid.at[:, rows], hid_sem.at[i])

    for i in range(n_chunk):
        hid_copy(i).start()

    barrier = pltpu.get_barrier_semaphore()
    for k in range(1, N_DP):
        pl.semaphore_signal(
            barrier, inc=1, device_id={"dp": zto(k)}, device_id_type=pl.DeviceIdType.MESH
        )
    for k in range(1, N_TP):
        pl.semaphore_signal(
            barrier,
            inc=1,
            device_id={"tensor": (t + k) % N_TP},
            device_id_type=pl.DeviceIdType.MESH,
        )
    pl.semaphore_wait(barrier, N_DP + N_TP - 2)

    lane = lax.broadcasted_iota(jnp.int32, (32, 128), 1)
    for i in range(n_chunk):
        hid_copy(i).wait()

        @pl.loop(0, CHUNK // 32)
        def _(r, i=i):
            rows = pl.ds(pl.multiple_of(i * CHUNK + r * 32, 32), 32)
            sums = []
            for layer in range(3):
                values = hid[layer, rows, :].astype(F32)
                sums.append(jnp.sum(values * values, axis=-1, keepdims=True))
            sqcol[rows, :] = jnp.where(
                lane == 0, sums[0], jnp.where(lane == 1, sums[1], sums[2])
            )

    sqsend[...] = sqcol[...].T[:8]

    def sq(k):
        return send(
            sqsend,
            sqrecv.at[k - 1],
            sq_ss.at[k - 1],
            sq_rs.at[k - 1],
            {"tensor": (t + k) % N_TP},
        )

    for k in range(1, N_TP):
        sq(k).start()
    seg_count = N_DP * SEG_DEV
    all_tokens = N_DP * tokens
    square = (seg_count, seg_count)
    owner_row = owner_ref[...].astype(F32)
    across = jnp.broadcast_to(owner_row, square)
    earlier = lax.broadcasted_iota(jnp.int32, square, 0) < lax.broadcasted_iota(
        jnp.int32, square, 1
    )
    match = jnp.where(earlier, jnp.where(across == across.T, 1.0, 0.0), 0.0)
    dest_seg = owner_row * SEG_DEV + jnp.sum(match, axis=0, keepdims=True)
    sub = lax.broadcasted_iota(jnp.int32, (8, seg_count), 0)
    rows8 = jnp.where(
        sub == 0,
        dest_seg,
        jnp.where(sub == 1, count_ref[...].astype(F32), length_ref[...].astype(F32)),
    ).astype(BF16)

    def spread(first, width):
        shape = (seg_count, width)
        token_seg = lax.broadcasted_iota(jnp.int32, shape, 1) // SEG + first
        hot = jnp.where(lax.broadcasted_iota(jnp.int32, shape, 0) == token_seg, 1.0, 0.0)
        return jnp.dot(rows8, hot.astype(BF16), preferred_element_type=F32)

    whole = spread(0, all_tokens)
    place = (lax.broadcasted_iota(jnp.int32, (1, all_tokens), 1) % SEG).astype(F32)
    dest[...] = whole[0:1] * SEG + place
    scale_row = whole[1:2] * mask_ref[...].astype(F32)
    scale_rows = jnp.broadcast_to(scale_row, (128, all_tokens)).astype(BF16)
    here = spread(z * SEG_DEV, tokens)
    live = jnp.where(place[:, :tokens] < here[2:3], 1.0, 0.0)

    def fill_order(first, count):
        @pl.loop(0, count // 32)
        def _(r):
            for half in range(2):
                start = pl.multiple_of(first + r * 32 + half * 16, 16)
                ids = lax.broadcasted_iota(jnp.int32, (16, 128), 0) + start
                ids = ids.astype(F32)
                for piece in range(all_tokens // 128):
                    cols = pl.ds(piece * 128, 128)
                    order[pl.ds(start, 16), cols] = jnp.where(
                        dest[:, cols] == ids, 1.0, 0.0
                    ).astype(BF16)

    fill_order(z * tokens, tokens)

    decay = decay_ref[...]
    positions = lax.broadcasted_iota(jnp.int32, (CHUNK, share), 0) % SEG

    def down(values):
        return jnp.where(positions == 0, 0.0, pltpu.roll(values, 1, 0))

    def up(values):
        return jnp.where(positions == SEG - 1, 0.0, pltpu.roll(values, CHUNK - 1, 0))

    for r in range(n_chunk):
        rows = pl.ds(r * CHUNK, CHUNK)
        mine = pl.ds(pl.multiple_of(z * tokens + r * CHUNK, CHUNK), CHUNK)
        scale = lax.dot_general(
            order[mine, :], scale_rows, (((1,), (1,)), ((), ())), preferred_element_type=F32
        )
        scale = jnp.concatenate([scale] * (share // 128), axis=1)
        third = cotangent_ref[2, rows, :].astype(F32) * scale
        second = cotangent_ref[1, rows, :].astype(F32) * scale + decay * up(third)
        first = cotangent_ref[0, rows, :].astype(F32) * scale + decay * up(second)
        total = (first + second + third).astype(BF16)
        grads[rows, :] = total
        gbuf[z, rows, lanes(t, share)] = total

    def g_block(zi, ti):
        return gbuf.at[zi, :, lanes(ti, share)]

    def gz(side, hop):
        step = 1 - 2 * side
        src = z - step * hop
        block = g_block(src, t)
        return send(
            grads if hop == 0 else block,
            block,
            gz_ss.at[side, hop],
            gz_rs.at[side, hop],
            {"dp": z + step},
        )

    def gx(d):
        block = g_block(d, t)
        return send(block, block, gx_ss.at[d], gx_rs.at[d], {"tensor": t_x})

    def gc(d):
        block = g_block(d, t)
        return send(block, block, gc_ss.at[d], gc_rs.at[d], {"tensor": t_c})

    def gxc(d):
        block = g_block(d, t_x)
        return send(block, block, gc_ss.at[4 + d], gc_rs.at[4 + d], {"tensor": t_c})

    def gz_arrived(side, hop):
        step = 1 - 2 * side
        block = g_block(z - step * hop, t)
        return send(
            block, block, gz_ss.at[side, hop - 1], gz_rs.at[side, hop - 1], {"dp": z - step}
        )

    def gx_arrived(d):
        block = g_block(d, t_x)
        return send(block, block, gx_ss.at[d], gx_rs.at[d], {"tensor": t_x})

    def gc_arrived(k, ti):
        block = g_block(k % 4, ti)
        return send(block, block, gc_ss.at[k], gc_rs.at[k], {"tensor": t_c})

    def came(side, hop):
        return z >= hop if side == 0 else z + hop < N_DP

    def goes(side, hop):
        return came(side, hop) & (z < N_DP - 1 if side == 0 else z > 0)

    def pass_on(hop):
        for side in range(2):

            @pl.when(goes(side, hop))
            def _(side=side):
                gz(side, hop).start()

    pass_on(0)
    gx(z).start()
    gc(z).start()

    def relay(hop):
        for side in range(2):

            @pl.when(came(side, hop))
            def _(side=side):
                gz_arrived(side, hop).wait_recv()

        if hop < N_DP - 1:
            pass_on(hop)
        for side in range(2):

            @pl.when(came(side, hop))
            def _(side=side):
                src = z - (1 - 2 * side) * hop
                gx(src).start()
                gc(src).start()

    for k in range(1, N_TP):
        sq(k).wait_recv()
    total = sqsend[...] + sqrecv[0] + sqrecv[1] + sqrecv[2]
    inverse = lax.rsqrt(total / D + epsilon) * live
    invcol[...] = jnp.concatenate([inverse, jnp.zeros((120, tokens), F32)], axis=0).T

    def jsend(k, i):
        rows = pl.ds(i * CHUNK, CHUNK)
        return send(
            jloc.at[k - 1, rows],
            jfeat.at[pl.ds(pl.multiple_of(z * tokens + i * CHUNK, CHUNK), CHUNK)],
            j_ss.at[k - 1, i],
            j_rs.at[k - 1, i],
            {"dp": zto(k)},
        )

    def jarrived(k, i):
        rows = pl.ds(pl.multiple_of(zfrom(k) * tokens + i * CHUNK, CHUNK), CHUNK)
        return send(
            jfeat.at[rows], jfeat.at[rows], j_ss.at[k - 1, i], j_rs.at[k - 1, i], {"dp": zto(k)}
        )

    for i in range(n_chunk):

        @pl.loop(0, CHUNK // 16)
        def _(r, i=i):
            rows = pl.ds(pl.multiple_of(i * CHUNK + r * 16, 16), 16)
            mine = pl.ds(pl.multiple_of(z * tokens + i * CHUNK + r * 16, 16), 16)
            table = invcol[rows, :]
            factors = [
                jnp.broadcast_to(table[:, layer : layer + 1], (16, 128)) for layer in range(3)
            ]
            for k in range(N_DP):
                for piece in range(feats // 128):
                    cols = pl.ds(pl.multiple_of(zto(k) * feats + piece * 128, 128), 128)
                    mixture = jnp.zeros((16, 128), F32)
                    for layer in range(3):
                        scaled = hid[layer, rows, cols].astype(F32) * gain_ref[layer : layer + 1, cols]
                        mixture = mixture + scaled * factors[layer]
                    out = pl.ds(piece * 128, 128)
                    if k:
                        jloc[k - 1, rows, out] = mixture.astype(BF16)
                    else:
                        jfeat[mine, out] = mixture.astype(BF16)

        for k in range(1, N_DP):
            jsend(k, i).start()
        if i == 2:
            relay(1)

    n_unit = N_DP * n_chunk

    def unit_rows(u):
        far = jnp.where(u < n_chunk, 0, (u + 3 * N_DP - n_chunk) % (N_DP - 1) + 1)
        part = jnp.where(u < n_chunk, u, (u + 3 * N_DP - n_chunk) // (N_DP - 1) - N_DP)
        return far, part, pl.multiple_of(zfrom(far) * tokens + part * CHUNK, CHUNK)

    def kc(u):
        return send(psend.at[u], precv.at[u], kc_ss.at[u], kc_rs.at[u], {"tensor": t_c})

    def kx(u):
        return send(xsend.at[u], xrecv.at[u], kx_ss.at[u], kx_rs.at[u], {"tensor": t_x})

    def project(u):
        _, _, start = unit_rows(u)
        block = jfeat[pl.ds(start, CHUNK), :]
        for half in range(2):
            other = weight_ref[:, lanes(2 * half + 1 - c, share)]
            psend[u, half] = jnp.dot(block, other, preferred_element_type=F32).astype(BF16)
        kc(u).start()
        for half in range(2):
            own = weight_ref[:, lanes(2 * half + c, share)]
            pown[u, half] = jnp.dot(block, own, preferred_element_type=F32)

    def along_x(u):
        kc(u).wait_recv()
        _, _, start = unit_rows(u)
        xsend[u] = (pown[u, 1 - x] + precv[u, 1 - x].astype(F32)).astype(BF16)
        kx(u).start()
        keys[pl.ds(start, CHUNK), :] = pown[u, x] + precv[u, x].astype(F32)

    def along_x_done(u):
        kx(u).wait_recv()
        _, _, start = unit_rows(u)
        mine = pl.ds(start, CHUNK)
        keysb[mine, :] = (keys[mine, :] + xrecv[u].astype(F32)).astype(BF16)

    for k in range(1, N_DP):
        fill_order(zto(k) * tokens, tokens)

    @pl.loop(0, n_unit + 2)
    def _(step):
        @pl.when((step >= n_chunk) & (step < n_unit))
        def _():
            far, part, _ = unit_rows(step)
            jarrived(far, part).wait_recv()

        @pl.when(step < n_unit)
        def _():
            project(step)

        for hop in (2, 3):

            @pl.when(step == 5 * hop + 2)
            def _(hop=hop):
                relay(hop)

        @pl.when((step >= 1) & (step <= n_unit))
        def _():
            along_x(step - 1)

        @pl.when(step >= 2)
        def _():
            along_x_done(step - 2)

    def kz(side, o):
        return send(
            ksend.at[o],
            krecv.at[side, o],
            kz_ss.at[side, o],
            kz_rs.at[side, o],
            {"dp": z + 1 - 2 * side},
        )

    def kz_arrived(side, o):
        return send(
            ksend.at[o],
            krecv.at[side, o],
            kz_ss.at[side, o],
            kz_rs.at[side, o],
            {"dp": z - 1 + 2 * side},
        )

    def own_part(o):
        return jnp.dot(
            order[o * tokens : (o + 1) * tokens, :], keysb[...], preferred_element_type=F32
        )

    last = N_DP - 1

    @pl.when(z == 0)
    def _():
        for o in (3, 2, 1):
            ksend[o] = own_part(o).astype(BF16)
            kz(0, o).start()
        kpart[0] = own_part(0)

    @pl.when(z == last)
    def _():
        for o in (0, 1, 2):
            ksend[o] = own_part(o).astype(BF16)
            kz(1, o).start()
        kpart[3] = own_part(3)

    @pl.when((z > 0) & (z < last))
    def _():
        for o in range(N_DP):
            kpart[o] = own_part(o)

    def stage(j):
        for side, o in ((0, last - j), (1, j)):

            @pl.when((z > 0) & (z < last) & (z < o if side == 0 else z > o))
            def _(side=side, o=o):
                kz_arrived(side, o).wait_recv()
                ksend[o] = (kpart[o] + krecv[side, o].astype(F32)).astype(BF16)
                kz(side, o).start()

    @pl.loop(0, 2 * N_DP)
    def _(b):
        rows = pl.ds(pl.multiple_of(b * (tokens // 2), tokens // 2), tokens // 2)
        jown[rows, :] = jnp.dot(
            order[rows, :], jfeat[...], preferred_element_type=F32
        ).astype(BF16)

    stage(0)

    @pl.loop(0, N_DP * n_chunk)
    def _(b):
        block = pl.ds(pl.multiple_of(b * CHUNK, CHUNK), CHUNK)
        jturn[:, block] = jown[block, :].T

    stage(1)
    for d in range(N_DP):
        gx_arrived(d).wait_recv()
        gxc(d).start()

    for k in range(N_DP):
        gc_arrived(k, t_c).wait_recv()
        gc_arrived(4 + k, t_xc).wait_recv()
    for n in range(N_TP):
        if n == 2:
            stage(2)
        cols = pl.ds(n * share, share)

        @pl.loop(0, feats // CHUNK)
        def _(r, cols=cols):
            rows = pl.ds(pl.multiple_of(r * CHUNK, CHUNK), CHUNK)
            value = jnp.zeros((CHUNK, share), F32)
            for d in range(N_DP):
                value = value + jnp.dot(
                    jturn[rows, pl.ds(d * tokens, tokens)],
                    gbuf[d, :, cols],
                    preferred_element_type=F32,
                )
            wgrad_ref[rows, cols] = value

    @pl.when(z > 0)
    def _():
        kz_arrived(0, z).wait_recv()
        kpart[z] = kpart[z] + krecv[0, z].astype(F32)

    @pl.when(z < last)
    def _():
        kz_arrived(1, z).wait_recv()
        kpart[z] = kpart[z] + krecv[1, z].astype(F32)

    @pl.loop(0, n_chunk)
    def _(r):
        rows = pl.ds(pl.multiple_of(r * CHUNK, CHUNK), CHUNK)
        value = kpart[z, rows, :]
        second = value + decay * down(value)
        third = value + decay * down(second)
        states_ref[0, rows, :] = value.astype(BF16)
        states_ref[1, rows, :] = second.astype(BF16)
        states_ref[2, rows, :] = third.astype(BF16)

    for k in range(1, N_DP):
        sq(k).wait_send()
        for i in range(n_chunk):
            jsend(k, i).wait_send()
    for hop in range(N_DP - 1):
        for side in range(2):

            @pl.when(goes(side, hop))
            def _(side=side, hop=hop):
                gz(side, hop).wait_send()

    for d in range(N_DP):
        gx(d).wait_send()
        gc(d).wait_send()
        gxc(d).wait_send()

        @pl.when(z < d)
        def _(d=d):
            kz(0, d).wait_send()

        @pl.when(z > d)
        def _(d=d):
            kz(1, d).wait_send()

    @pl.loop(0, n_unit)
    def _(u):
        kc(u).wait_send()
        kx(u).wait_send()


def fused(
    hidden_rows,
    layer_gain,
    key_weight,
    step_decay,
    owner_list,
    segment_len,
    reweight_count,
    loss_mask,
    state_cotangent,
):
    share = state_cotangent.shape[3]
    tokens, layers, width = hidden_rows.shape
    feats, key_width = key_weight.shape

    vmem = pl.BlockSpec(memory_space=pltpu.VMEM)
    dma = pltpu.SemaphoreType.DMA
    n_chunk = tokens // CHUNK
    n_unit = N_DP * n_chunk
    states, weight_grad = pl.pallas_call(
        fused_kernel,
        out_shape=(
            jax.ShapeDtypeStruct((3, tokens, share), BF16),
            jax.ShapeDtypeStruct((feats, key_width), F32),
        ),
        in_specs=[
            vmem,
            vmem,
            vmem,
            vmem,
            pl.BlockSpec(memory_space=pl.ANY),
            vmem,
            vmem,
            vmem,
            vmem,
        ],
        out_specs=(vmem, vmem),
        scratch_shapes=[
            pltpu.VMEM((layers, tokens, width), BF16),
            pltpu.VMEM((1, N_DP * tokens), F32),
            pltpu.VMEM((tokens, share), BF16),
            pltpu.VMEM((tokens, 128), F32),
            pltpu.VMEM((8, tokens), F32),
            pltpu.VMEM((3, 8, tokens), F32),
            pltpu.VMEM((tokens, 128), F32),
            pltpu.VMEM((3, tokens, feats), BF16),
            pltpu.VMEM((N_DP * tokens, feats), BF16),
            pltpu.VMEM((N_DP * tokens, feats), BF16),
            pltpu.VMEM((feats, N_DP * tokens), BF16),
            pltpu.VMEM((N_DP * tokens, N_DP * tokens), BF16),
            pltpu.VMEM((N_DP, tokens, key_width), BF16),
            pltpu.VMEM((n_unit, 2, CHUNK, share), BF16),
            pltpu.VMEM((n_unit, 2, CHUNK, share), BF16),
            pltpu.VMEM((n_unit, 2, CHUNK, share), F32),
            pltpu.VMEM((n_unit, CHUNK, share), BF16),
            pltpu.VMEM((n_unit, CHUNK, share), BF16),
            pltpu.VMEM((N_DP * tokens, share), F32),
            pltpu.VMEM((N_DP * tokens, share), BF16),
            pltpu.VMEM((N_DP, tokens, share), F32),
            pltpu.VMEM((N_DP, tokens, share), BF16),
            pltpu.VMEM((2, N_DP, tokens, share), BF16),
            dma((n_chunk,)),
            dma((3,)),
            dma((3,)),
            dma((3, n_chunk)),
            dma((3, n_chunk)),
            dma((2, 3)),
            dma((2, 3)),
            dma((4,)),
            dma((4,)),
            dma((8,)),
            dma((8,)),
            dma((n_unit,)),
            dma((n_unit,)),
            dma((n_unit,)),
            dma((n_unit,)),
            dma((2, 4)),
            dma((2, 4)),
        ],
        compiler_params=pltpu.CompilerParams(
            collective_id=0, has_side_effects=True, vmem_limit_bytes=60 * 1024 * 1024
        ),
        cost_estimate=pl.CostEstimate(
            flops=4 * N_DP * tokens * feats * key_width,
            bytes_accessed=12 * 1024 * 1024,
            transcendentals=0,
        ),
        name="draft_head",
    )(
        owner_list.reshape(1, -1),
        segment_len.reshape(1, -1),
        reweight_count.reshape(1, -1),
        loss_mask.reshape(1, -1),
        hidden_rows.transpose(1, 0, 2),
        layer_gain,
        key_weight,
        step_decay.reshape(1, share),
        state_cotangent.reshape(3, tokens, share),
    )
    return (states.reshape(3, SEG_DEV, SEG, share), weight_grad)


def uses_kernel(mesh):
    return mesh.shape["dp"] == N_DP and mesh.shape["tensor"] == N_TP


def solution(mesh):
    return jax.shard_map(
        fused if uses_kernel(mesh) else per_device,
        mesh=mesh,
        in_specs=(
            P(("groups", "dp"), None, "tensor"),
            P(None, "tensor"),
            P(("tensor", "dp"), None),
            P("tensor"),
            P("groups"),
            P("groups"),
            P("groups"),
            P("groups"),
            P(None, ("groups", "dp"), None, "tensor"),
        ),
        out_specs=(P(None, ("groups", "dp"), None, "tensor"), P(("groups", "tensor", "dp"), None)),
        check_vma=False,
    )
```
